128 devices in a mesh: tok: 16 (over z, x), head: 8 (over y, core).
Axes of the slice: x: 4, y: 4, z: 4, core: 2. Of those that a mesh axis runs over, the one named last changes fastest.
Arguments:
- query_tokens: bfloat16 [2, 4096, 5120], P(None, ('tok', 'head')), may hold values from -6 to 6
- key_tokens: bfloat16 [2, 4096, 5120], P(None, ('tok', 'head')), may hold values from -6 to 6
- value_tokens: bfloat16 [2, 4096, 5120], P(None, ('tok', 'head')), may hold values from -6 to 6
- out_grad: bfloat16 [2, 4096, 5120], P(None, ('tok', 'head')), may hold values from -6 to 6
- fast_init: float32 [3, 16, 320, 320], P(None, 'head'), may hold values from -0.3125 to 0.3125
Outputs:
- query_grad: bfloat16 [2, 4096, 5120], P(None, ('tok', 'head'))
- key_grad: bfloat16 [2, 4096, 5120], P(None, ('tok', 'head'))
- value_grad: bfloat16 [2, 4096, 5120], P(None, ('tok', 'head'))
- fast_grad: float32 [3, 16, 320, 320], P(None, 'head')
The draws below stay inside these ranges and needn't reach their ends.
All inputs are finite; a program needn't handle non-finite values.
Results may differ from the reference program's by a relative error of at most 0.009.
Values may be sent and summed in bfloat16 or wider, within the bound.
No kernel may reach another device: no remote copies, remote signals or barrier semaphores. Data moves between devices by JAX's collectives and lax.ppermute only.
A program may use at most 128 MiB of HBM per device.

```python
import math
import jax
import jax.numpy as jnp
from jax import lax

DH = 320
HEADS = 16
NCH = 2
SPAN = 4096
WIDTH = 5120


def levels(stream_key, shape, cuts, low, high):
    def one(position, parts):
        draws = jax.random.uniform(jax.random.fold_in(jax.random.fold_in(stream_key, 6), position), (parts,), jnp.float32, low / len(cuts), high / len(cuts))
        return jnp.repeat(jnp.exp(draws), shape[position] // parts).reshape((-1,) + (1,) * (len(shape) - position - 1))

    factor_of = one(*cuts[0])
    for cut in cuts[1:]:
        factor_of = factor_of * one(*cut)
    return factor_of


def centred(own_key, extent, deviation, bound, shards=(), held_as=jnp.bfloat16):
    values = jax.random.normal(own_key, extent, jnp.float32) * deviation
    if len(shards) > 0:
        values = levels(own_key, extent, shards, -0.22, 0.18) * values
    return jnp.clip(values, min=-bound, max=bound).astype(held_as)


def setup_inputs(seed: int = 0) -> dict:
    arg_keys = jax.random.split(jax.random.key(seed), 6)
    query_tokens = centred(arg_keys[0], (NCH, SPAN, WIDTH), 1.0, 6.0, ((1, 128),))
    key_tokens = centred(arg_keys[1], (NCH, SPAN, WIDTH), 1.0, 6.0, ((1, 128),))
    value_tokens = centred(arg_keys[2], (NCH, SPAN, WIDTH), 1.0, 6.0, ((1, 128),))
    out_grad = centred(arg_keys[3], (NCH, SPAN, WIDTH), 1.0, 6.0, ((1, 128),))
    fast_init = centred(arg_keys[4], (3, HEADS, DH, DH), DH ** -0.5, 0.3125, ((1, 8),), jnp.float32)
    return {"query_tokens": query_tokens, "key_tokens": key_tokens, "value_tokens": value_tokens, "out_grad": out_grad, "fast_init": fast_init}


eps_norm = 1e-06

def product(left, right):
    return jnp.dot(left, right, precision=lax.Precision.HIGHEST, preferred_element_type=jnp.float32)

def contract(left, right):
    return lax.dot_general(left, right, (((0,), (0,)), ((), ())), precision=lax.Precision.HIGHEST, preferred_element_type=jnp.float32)

def silu_parts(inputs):
    sigmoid_z = jax.nn.sigmoid(inputs)
    first_slope = sigmoid_z * (1.0 + inputs * (1.0 - sigmoid_z))
    second_slope = sigmoid_z * (1.0 - sigmoid_z) * (2.0 + inputs * (1.0 - 2.0 * sigmoid_z))
    return (inputs * sigmoid_z, first_slope, second_slope)

def update_terms(key_rows, value_rows, w_gate, w_up, w_down):
    z_one = product(key_rows, w_gate)
    z_three = product(key_rows, w_up)
    silu_out, first_slope, second_slope = silu_parts(z_one)
    hidden = silu_out * z_three
    out_error = -product(value_rows, w_down.T)
    f_three = out_error * silu_out
    f_one = out_error * z_three * first_slope
    gradient = (contract(key_rows, f_one), contract(key_rows, f_three), -contract(hidden, value_rows))
    return (gradient, (z_three, silu_out, first_slope, second_slope, hidden, out_error, f_one, f_three))

def readout_terms(query_rows, upstream, w_gate, w_up, w_down):
    y_one = product(query_rows, w_gate)
    y_three = product(query_rows, w_up)
    silu_out, first_slope, second_slope = silu_parts(y_one)
    back_hidden = product(upstream, w_down.T)
    d_one = back_hidden * y_three * first_slope
    d_three = back_hidden * silu_out
    query_part = product(d_one, w_gate.T) + product(d_three, w_up.T)
    sums = (contract(query_rows, d_one), contract(query_rows, d_three), contract(silu_out * y_three, upstream))
    return (query_part, sums)

def cotangent(total, gradient, scale, entries, step_size):
    return -step_size * (total / scale - gradient * jnp.sum(total * gradient) / (entries * scale * scale * scale))

def second_terms(key_rows, value_rows, saved, w_gate, w_up, w_down, cot_gate, cot_up, cot_down):
    z_three, silu_out, first_slope, second_slope, hidden, out_error, f_one, f_three = saved
    bar_one = product(key_rows, cot_gate)
    bar_three = product(key_rows, cot_up)
    bar_hidden = -product(value_rows, cot_down.T)
    key_part = product(f_one, cot_gate.T) + product(f_three, cot_up.T)
    value_part = -product(hidden, cot_down)
    bar_error = bar_three * silu_out + bar_one * z_three * first_slope
    bar_silu = bar_three * out_error + bar_hidden * z_three
    bar_zthree = bar_one * out_error * first_slope + bar_hidden * silu_out
    bar_zone = bar_one * out_error * z_three * second_slope + bar_silu * first_slope
    value_part = value_part - product(bar_error, w_down)
    key_part = key_part + product(bar_zone, w_gate.T) + product(bar_zthree, w_up.T)
    sums = (contract(key_rows, bar_zone), contract(key_rows, bar_zthree), -contract(bar_error, value_rows))
    return (key_part, value_part, sums)

def head_pass(query_h, key_h, value_h, upstream_h, fast_h):
    dim = fast_h.shape[1]
    entries = dim * dim
    step_size = 0.25 / math.sqrt(dim)
    spans = query_h.shape[0]
    weights = [(fast_h[0], fast_h[1], fast_h[2])]
    gradients, scales, saves = ([], [], [])
    for which in range(spans):
        gradient, saved = update_terms(key_h[which].astype(jnp.float32), value_h[which].astype(jnp.float32), *weights[-1])
        scale = tuple((jnp.sqrt(jnp.sum(part * part) / entries + eps_norm) for part in gradient))
        weights.append(tuple((old - step_size * part / size for old, part, size in zip(weights[-1], gradient, scale))))
        gradients.append(gradient)
        scales.append(scale)
        saves.append(saved)
    carry = tuple((jnp.zeros((dim, dim), jnp.float32) for part in range(3)))
    query_out, key_out, value_out = ([None] * spans, [None] * spans, [None] * spans)
    for which in reversed(range(spans)):
        query_part, readout = readout_terms(query_h[which].astype(jnp.float32), upstream_h[which].astype(jnp.float32), *weights[which + 1])
        total = tuple((first + second for first, second in zip(readout, carry)))
        cots = tuple((cotangent(tot, grad, size, entries, step_size) for tot, grad, size in zip(total, gradients[which], scales[which])))
        key_part, value_part, sums = second_terms(key_h[which].astype(jnp.float32), value_h[which].astype(jnp.float32), saves[which], *weights[which], *cots)
        carry = tuple((first + second for first, second in zip(total, sums)))
        query_out[which] = query_part.astype(jnp.bfloat16)
        key_out[which] = key_part.astype(jnp.bfloat16)
        value_out[which] = value_part.astype(jnp.bfloat16)
    return (jnp.stack(query_out), jnp.stack(key_out), jnp.stack(value_out), jnp.stack(carry))

def reference(query_tokens, key_tokens, value_tokens, out_grad, fast_init):

    def split(array):
        return jnp.transpose(array.reshape(NCH, SPAN, HEADS, DH), (2, 0, 1, 3))

    def merge(array):
        return jnp.transpose(array, (1, 2, 0, 3)).reshape(NCH, SPAN, HEADS * DH)
    fast = jnp.transpose(fast_init, (1, 0, 2, 3))
    query_all, key_all, value_all, fast_all = lax.map(lambda items: head_pass(*items), (split(query_tokens), split(key_tokens), split(value_tokens), split(out_grad), fast))
    return (merge(query_all), merge(key_all), merge(value_all), jnp.transpose(fast_all, (1, 0, 2, 3)))
```

```python
import math

import jax
import jax.numpy as jnp
from jax import lax
from jax.experimental import pallas as pl
from jax.experimental.pallas import tpu as pltpu
from jax.sharding import Mesh, PartitionSpec as P

BF = jnp.bfloat16
F32 = jnp.float32
EPS = 1e-06
D = 320
LANES = 128
MAT = 800
CHUNK = 304
HALF = 4 * CHUNK
FULL = 8 * CHUNK
ROWS = 32
PACK = 80
PEERS = 16
TOK = PEERS * ROWS
TILE = 128

X = ("x1", "x0")
C = ("c",)
YZ = ("y1", "y0", "z1", "z0")
EVERY = ("z1", "z0", "x1", "x0", "y1", "y0", "c")
ROOMY = pltpu.CompilerParams(vmem_limit_bytes=60 * 1024 * 1024)
PARAMS = pltpu.CompilerParams(vmem_limit_bytes=40 * 1024 * 1024)


def nn(a, b):
    return lax.dot_general(a, b, (((1,), (0,)), ((), ())), preferred_element_type=F32)


def nt(a, b):
    return lax.dot_general(a, b, (((1,), (1,)), ((), ())), preferred_element_type=F32)


def tn(a, b):
    return lax.dot_general(a, b, (((0,), (0,)), ((), ())), preferred_element_type=F32)


def put_tokens(out, head, off, rows):
    out[head, off : off + 32, :] = rows[:, 0:128]
    out[head, off + 32 : off + 64, :] = rows[:, 128:256]
    out[head, off + 64 : off + 80, :] = jnp.concatenate([rows[0:16, 256:320], rows[16:32, 256:320]], axis=1)


def get_tokens(ref, off, dst):
    dst[:, 0:128] = ref[:, off : off + 32, :].reshape(TOK, 128)
    dst[:, 128:256] = ref[:, off + 32 : off + 64, :].reshape(TOK, 128)
    tail = ref[:, off + 64 : off + 80, :]
    both = jnp.concatenate([tail[:, :, 0:64], tail[:, :, 64:128]], axis=1)
    dst[:, 256:320] = both.reshape(TOK, 64)


def put_token_grad(out, off, value):
    value = value.astype(BF)
    out[:, off : off + 32, :] = value[:, 0:128].reshape(PEERS, 32, 128)
    out[:, off + 32 : off + 64, :] = value[:, 128:256].reshape(PEERS, 32, 128)
    tail = value[:, 256:320].reshape(PEERS, 32, 64)
    out[:, off + 64 : off + 80, :] = jnp.concatenate([tail[:, 0:16, :], tail[:, 16:32, :]], axis=2)


def put_matrix(flat, which, m):
    base = which * MAT
    flat[base : base + 320, :] = m[:, 0:128]
    flat[base + 320 : base + 640, :] = m[:, 128:256]
    flat[base + 640 : base + 800, :] = jnp.concatenate([m[0:160, 256:320], m[160:320, 256:320]], axis=1)


def get_matrix(flat, which):
    base = which * MAT
    tail = flat[base + 640 : base + 800, :]
    last = jnp.concatenate([tail[:, 0:64], tail[:, 64:128]], axis=0)
    return jnp.concatenate([flat[base : base + 320, :], flat[base + 320 : base + 640, :], last], axis=1)


def clear_tail(flat):
    flat[3 * MAT : FULL, :] = jnp.zeros((FULL - 3 * MAT, 128), F32)


def split_out(flat, place, send, keep):
    core = place[0]
    send[...] = flat[pl.ds(pl.multiple_of((1 - core) * HALF, 16), HALF), :].astype(BF)
    keep[...] = flat[pl.ds(pl.multiple_of(core * HALF, 16), HALF), :]


def join_in(flat, place, parts):
    core, x = place[0], place[1]
    for k in range(4):
        at = lax.rem(x + 4 - k, 4) * CHUNK
        for half, part in ((core, parts[k]), (1 - core, parts[4 + k])):
            rows = pl.ds(pl.multiple_of(half * HALF + at, 16), CHUNK)
            flat[rows, :] = part[...].astype(F32)


def sigmoid(z):
    return 0.5 + 0.5 * jnp.tanh(0.5 * z)


def scale_of(g):
    return jnp.sqrt(jnp.sum(g * g) / (D * D) + EPS)


def rows_of(t):
    return pl.ds(pl.multiple_of(t * TILE, TILE), TILE)


def mat(ref, m):
    return ref[m * D : m * D + D, :]


def set_mat(ref, m, value):
    ref[m * D : m * D + D, :] = value


def set_halves(pair, m, w):
    high = w.astype(BF)
    set_mat(pair, m, high)
    set_mat(pair, 3 + m, (w - high.astype(F32)).astype(BF))


def nn2(a, pair, m):
    return nn(a, mat(pair, m)) + nn(a, mat(pair, 3 + m))


def nt2(a, pair, m):
    return nt(a, mat(pair, m)) + nt(a, mat(pair, 3 + m))


def over_tiles(step):
    def body(t, carry):
        step(rows_of(t))
        return carry

    lax.fori_loop(0, TOK // TILE, body, 0, unroll=True)


def update_body(moves, first, k, v, wp, s_out, p_out, q_out, r_out, f1, f3, hd, flat):
    def step(rows):
        kt, vt = k[rows, :], v[rows, :]
        z1, z3, e = nn2(kt, wp, 0), nn2(kt, wp, 1), -nt2(vt, wp, 2)
        sig = sigmoid(z1)
        s = z1 * sig
        rest = 1.0 - sig
        s1 = sig * (1.0 + z1 * rest)
        s2 = sig * rest * (2.0 + z1 * (1.0 - 2.0 * sig))
        p = z3 * s1
        s_out[rows, :] = s
        p_out[rows, :] = p
        q_out[rows, :] = e * s1
        r_out[rows, :] = e * z3 * s2
        f1[rows, :] = (e * p).astype(BF)
        f3[rows, :] = (e * s).astype(BF)
        hd[rows, :] = (s * z3).astype(BF)
        moves.flush_rows(first, rows)

    over_tiles(step)
    put_matrix(flat, 0, tn(k[...], f1[...]))
    put_matrix(flat, 1, tn(k[...], f3[...]))
    put_matrix(flat, 2, -tn(hd[...], v[...]))
    clear_tail(flat)


def readout_tiles(q, u, wp, d1, d3, td, ready=lambda rows: None):
    def step(rows):
        qt, ut = q[rows, :], u[rows, :]
        y1, y3, d = nn2(qt, wp, 0), nn2(qt, wp, 1), nt2(ut, wp, 2)
        sig = sigmoid(y1)
        s = y1 * sig
        s1 = sig * (1.0 + y1 * (1.0 - sig))
        d1[rows, :] = (d * y3 * s1).astype(BF)
        d3[rows, :] = (d * s).astype(BF)
        td[rows, :] = (s * y3).astype(BF)
        ready(rows)

    over_tiles(step)


def readout_sums(q, u, d1, d3, td):
    return tn(q[...], d1[...]), tn(q[...], d3[...]), tn(td[...], u[...])


def query_part(d1, d3, wp):
    return nt(d1[...], mat(wp, 0)) + nt(d3[...], mat(wp, 1))


def step_weights(w_old, flat, g_out, eta):
    for m in range(3):
        g = get_matrix(flat, m)
        set_mat(g_out, m, g.astype(BF))
        yield m, mat(w_old, m) - eta * (g / scale_of(g))


def first_weights_kernel(moves, place, held, got, w0):
    own = place[3] == 1
    for m in range(3):
        set_mat(w0, m, jnp.where(own, held[m], got[m]))


def first_update_kernel(moves, place, tokens, w0, send, keep, k, v, *refs):
    made, (wp, flat) = refs[:7], refs[7:]
    get_tokens(tokens, 0, k)
    get_tokens(tokens, PACK, v)
    moves.flush(2)
    moves.load()
    for m in range(3):
        set_halves(wp, m, mat(w0, m))
    update_body(moves, 2, k, v, wp, *made, flat)
    split_out(flat, place, send, keep)


def next_update_kernel(eta, moves, place, tokens, *refs):
    parts, (w0, send, keep, w1, g, k, v, *made, wp, flat) = refs[:8], refs[8:]
    join_in(flat, place, parts)
    get_tokens(tokens, 0, k)
    get_tokens(tokens, PACK, v)
    moves.load()
    for m, w in step_weights(w0, flat, g, eta):
        set_mat(w1, m, w)
        set_halves(wp, m, w)
    moves.flush(4)
    update_body(moves, 4, k, v, wp, *made, flat)
    split_out(flat, place, send, keep)


def first_readout_kernel(moves, tokens, w1, sums, grad, q, u, wp, d1, d3, td):
    moves.load()
    get_tokens(tokens, 4 * PACK, q)
    get_tokens(tokens, 5 * PACK, u)
    for m in range(3):
        set_halves(wp, m, mat(w1, m))
    readout_tiles(q, u, wp, d1, d3, td)
    for m, value in enumerate(readout_sums(q, u, d1, d3, td)):
        set_mat(sums, m, value)
    grad[...] = query_part(d1, d3, wp).astype(BF)


def last_readout_kernel(eta, moves, place, tokens, *refs):
    parts, (w1, send, keep, wp, g, d1, d3, q, u, td, flat) = refs[:8], refs[8:]
    join_in(flat, place, parts)
    get_tokens(tokens, 2 * PACK, q)
    get_tokens(tokens, 3 * PACK, u)
    moves.load()
    for m, w in step_weights(w1, flat, g, eta):
        set_halves(wp, m, w)
    moves.flush(2)
    readout_tiles(q, u, wp, d1, d3, td, lambda rows: moves.flush_rows(2, rows))
    for m, value in enumerate(readout_sums(q, u, d1, d3, td)):
        put_matrix(flat, m, value)
    clear_tail(flat)
    split_out(flat, place, send, keep)


def query_kernel(moves, d1, d3, wp, grad):
    moves.load()
    grad[...] = query_part(d1, d3, wp).astype(BF)


def second_kernel(eta, last, moves, place, *refs):
    parts, (g_in, extra, k, v, s_in, p_in, q_in, r_in, send, keep, pp, *refs) = refs[:8], refs[8:]
    total = None if last else refs[0]
    b1, b3, be, flat = refs[-4:]
    join_in(flat, place, parts)
    moves.load(2)
    for m in range(3):
        g = mat(g_in, m).astype(F32)
        p = get_matrix(flat, m)
        if last:
            p = p + mat(extra, m).astype(F32)
        else:
            set_mat(total, m, p.astype(BF))
        size = scale_of(g)
        along = jnp.sum(p * g) / (D * D * size * size * size)
        set_halves(pp, m, -eta * (p / size - g * along))
    done = 1 if last else 2
    moves.flush(done)
    moves.load()

    def step(rows):
        kt, vt = k[rows, :], v[rows, :]
        ba, bb, bh = nn2(kt, pp, 0), nn2(kt, pp, 1), -nt2(vt, pp, 2)
        s, p, q = s_in[rows, :], p_in[rows, :], q_in[rows, :]
        be[rows, :] = (bb * s + ba * p).astype(BF)
        b3[rows, :] = (ba * q + bh * s).astype(BF)
        b1[rows, :] = (ba * r_in[rows, :] + bb * q + bh * p).astype(BF)
        moves.flush_rows(done, rows)

    over_tiles(step)
    for m, value in enumerate((tn(k[...], b1[...]), tn(k[...], b3[...]), -tn(be[...], v[...]))):
        put_matrix(flat, m, value if last else value + mat(extra, m))
    clear_tail(flat)
    split_out(flat, place, send, keep)


def mix_kernel(place, keep, got, own, one, two, three):
    for k, out in enumerate((own, one, two, three)):
        rows = pl.ds(pl.multiple_of(lax.rem(place[1] + k, 4) * CHUNK, 16), CHUNK)
        out[...] = (keep[rows, :] + got[rows, :].astype(F32)).astype(out.dtype)


def add_kernel(*refs):
    total = refs[0][...].astype(F32)
    for ref in refs[1:-1]:
        total = total + ref[...].astype(F32)
    refs[-1][...] = total.astype(refs[-1].dtype)


def token_kernel(last, moves, *refs):
    if last:
        packed, pp, f1, f3, hd, w, b1, b3, be, grad, wp = refs
        grad[:, 2 * PACK : 6 * PACK, :] = packed[...]
    else:
        pp, f1, f3, hd, w, b1, b3, be, dq1, dq2, grad, wp = refs
    moves.load(4)
    key_part = nt2(f1[...], pp, 0) + nt2(f3[...], pp, 1)
    value_part = nn2(hd[...], pp, 2)
    moves.load()
    for m in range(3):
        set_halves(wp, m, mat(w, m))
    put_token_grad(grad, 0, key_part + nt2(b1[...], wp, 0) + nt2(b3[...], wp, 1))
    put_token_grad(grad, PACK, -(value_part + nn2(be[...], wp, 2)))
    if not last:
        put_token_grad(grad, 2 * PACK, dq2[...])
        put_token_grad(grad, 3 * PACK, dq1[...])


def unpack_kernel(plan, n_in, *refs):
    ins, outs = refs[:n_in], refs[n_in:]
    for where, block, which, off in plan:
        ref, out = ins[which], outs[where]
        for head in range(16):
            tail = ref[head, off + 64 : off + 80, :]
            last = jnp.concatenate([tail[:, 0:64], tail[:, 64:128]], axis=0)
            out[block, :, head * D : head * D + D] = jnp.concatenate(
                [ref[head, off : off + 32, :], ref[head, off + 32 : off + 64, :], last], axis=1
            )


def fast_kernel(place, a0, a1, a2, a3, out, flat):
    core, x = place[0], place[1]
    for k, part in enumerate((a0, a1, a2, a3)):
        at = lax.rem(x + 4 - k, 4) * CHUNK
        for head in range(2):
            for i, half in enumerate((core, 1 - core)):
                rows = pl.ds(pl.multiple_of(half * HALF + at, 16), CHUNK)
                flat[head, rows, :] = part[2 * i + head].astype(F32)
    for head in range(2):
        for m in range(3):
            out[m, head] = get_matrix(flat.at[head], m)


VM = pl.BlockSpec(memory_space=pltpu.VMEM)
SM = pl.BlockSpec(memory_space=pltpu.SMEM)
HB = pl.BlockSpec(memory_space=pltpu.HBM)


def tok_scratch(n):
    return [pltpu.VMEM((TOK, D), BF) for _ in range(n)]


MATS = (3, D, D)


def layout(least, **sizes):
    places, at = {}, 0
    for name, rows in sizes.items():
        places[name] = (at, rows)
        at += rows
    return places, max(at, least)


WIDE, WIDE_ROWS = layout(
    20480, s1=TOK, p1=TOK, q1=TOK, r1=TOK, s2=TOK, p2=TOK, q2=TOK, r2=TOK, w0=3 * D, w1=3 * D, sums=3 * D
)
SHORT, SHORT_ROWS = layout(
    40960, k1=TOK, v1=TOK, fa1=TOK, fb1=TOK, hd1=TOK, k2=TOK, v2=TOK, fa2=TOK, fb2=TOK, hd2=TOK,
    g1=3 * D, g2=3 * D, total=3 * D, ba=TOK, bb=TOK, be=TOK, pp=6 * D, w2=6 * D, da=TOK, db=TOK, dq1=TOK, dq2=TOK,
)


def slot(name):
    return (0, *WIDE[name]) if name in WIDE else (1, *SHORT[name])


class Moves:
    def __init__(self, ins, outs, pieces):
        self.ins, self.outs, self.flushed, self.pieces, self.by_rows = ins, outs, 0, pieces, False
        for copy in ins:
            copy.start()

    def load(self, count=None):
        for copy in self.ins[:count]:
            copy.wait()
        self.ins = [] if count is None else self.ins[count:]

    def flush_rows(self, first, rows):
        self.by_rows = True
        for stage, there, sem in self.pieces[first:]:
            pltpu.make_async_copy(stage.at[rows, :], there.at[rows, :], sem).start()

    def flush(self, count=None):
        for copy in self.outs[self.flushed : count]:
            copy.start()
        self.flushed = len(self.outs) if count is None else count

    def end(self):
        if self.flushed < len(self.outs) and not self.by_rows:
            self.flush()
        for copy in self.outs:
            copy.wait()


def worked(kernel, work, outs, scratch, *args, scalars=1, flops=0, near=(), far=()):
    near, far = list(near), list(far)
    n_in, n_out, n_scratch, n_work = len(args), len(outs), len(scratch), len(work)

    def wrapped(*refs):
        args, refs = refs[:n_in], refs[n_in + n_work :]
        results, held, refs = refs[:n_out], refs[n_out : n_out + 2], refs[n_out + 2 :]
        own, stages, sems = refs[:n_scratch], refs[n_scratch:-1], refs[-1]
        ins, outs, pieces = [], [], []
        for i, name in enumerate(near + far):
            which, at, rows = slot(name)
            there = held[which].at[pl.ds(at, rows), :]
            if i < len(near):
                ins.append(pltpu.make_async_copy(there, stages[i], sems.at[i]))
            else:
                outs.append(pltpu.make_async_copy(stages[i], there, sems.at[i]))
                pieces.append((stages[i], there, sems.at[i]))
        moves = Moves(ins, outs, pieces)
        kernel(moves, *args, *stages[: len(near)], *results, *stages[len(near) :], *own)
        moves.end()

    stages = []
    for name in near + far:
        which, _, rows = slot(name)
        stages.append(pltpu.VMEM((rows, D), BF if which else F32))
    spaces = [jax.ShapeDtypeStruct((WIDE_ROWS, D), F32), jax.ShapeDtypeStruct((SHORT_ROWS, D), BF)]
    *results, wide, short = pl.pallas_call(
        wrapped,
        out_shape=[jax.ShapeDtypeStruct(s, t) for s, t in outs] + spaces,
        in_specs=[SM if i < scalars else VM for i in range(n_in)] + [HB] * n_work,
        out_specs=[VM] * n_out + [HB] * 2,
        scratch_shapes=list(scratch) + stages + [pltpu.SemaphoreType.DMA((len(stages),))],
        input_output_aliases={n_in + i: n_out + i for i in range(n_work)},
        compiler_params=PARAMS,
        cost_estimate=pl.CostEstimate(flops=flops, bytes_accessed=4_000_000, transcendentals=TOK * D),
    )(*args, *work)
    return *results, (wide, short)


def call(kernel, outs, *args, scalars=1, scratch=()):
    return pl.pallas_call(
        kernel,
        out_shape=[jax.ShapeDtypeStruct(s, t) for s, t in outs],
        in_specs=[SM if i < scalars else VM for i in range(len(args))],
        out_specs=[VM] * len(outs),
        scratch_shapes=list(scratch),
        compiler_params=PARAMS,
    )(*args)


def pack(plan, *args):
    def kernel(*refs):
        ins, out, stage, sems = refs[: len(args)], refs[-3], refs[-2], refs[-1]
        pack_pieces(plan, ins, out, stage, sems)

    n = len(plan)
    return pl.pallas_call(
        kernel,
        out_shape=jax.ShapeDtypeStruct((PEERS, n * PACK, 128), BF),
        in_specs=[HB] * len(args),
        out_specs=VM,
        scratch_shapes=[pltpu.VMEM((n, ROWS, 16 * D), BF), pltpu.SemaphoreType.DMA((n,))],
        compiler_params=ROOMY,
    )(*args)


def pack_pieces(plan, ins, out, stage, sems):
    copies = [
        pltpu.make_async_copy(ins[which].at[block], stage.at[i], sems.at[i]) for i, (which, block) in enumerate(plan)
    ]
    for copy in copies:
        copy.start()
    for i, copy in enumerate(copies):
        copy.wait()
        for head in range(16):
            put_tokens(out, head, i * PACK, stage[i, :, head * D : head * D + D])


def pack_first(plan, place, fast_init, *args):
    def kernel(place, given, *refs):
        ins, (out, held, stage, sems) = refs[: len(args)], refs[-4:]
        n = len(plan)
        weights = [pltpu.make_async_copy(given.at[m, place[2]], held.at[m], sems.at[n + m]) for m in range(3)]
        for copy in weights:
            copy.start()
        pack_pieces(plan, ins, out, stage, sems)
        for copy in weights:
            copy.wait()

    n = len(plan)
    return pl.pallas_call(
        kernel,
        out_shape=[jax.ShapeDtypeStruct((PEERS, n * PACK, 128), BF), jax.ShapeDtypeStruct(MATS, F32)],
        in_specs=[SM] + [HB] * (1 + len(args)),
        out_specs=[VM, VM],
        scratch_shapes=[pltpu.VMEM((n, ROWS, 16 * D), BF), pltpu.SemaphoreType.DMA((n + 3,))],
        compiler_params=ROOMY,
    )(place, fast_init, *args)


SPLIT = [((HALF, 128), BF), ((HALF, 128), F32)]
FLAT = pltpu.VMEM((FULL, 128), F32)
WP = pltpu.VMEM((6 * D, D), BF)
UNIT = 2 * TOK * D * D


def exchange(a):
    return lax.all_to_all(a, YZ, 0, 0, tiled=True)


def cross(a):
    return lax.ppermute(a, C, [(0, 1), (1, 0)])


def turn(a, k):
    return lax.ppermute(a, X, [(i, (i + k) % 4) for i in range(4)])


PIECE = (CHUNK, 128)


def scatter(place, send, keep, *more):
    own, *rest = call(mix_kernel, [(PIECE, F32)] + [(PIECE, BF)] * 3, place, keep, cross(send))
    got = [turn(part, k) for k, part in zip((1, 2, 3), rest)]
    (chunk,) = call(add_kernel, [(PIECE, BF)], own, *got, *more, scalars=0)
    return chunk


def gather(chunk):
    mine = [chunk, turn(chunk, 1), turn(chunk, 2), turn(chunk, 3)]
    return mine + [cross(part) for part in mine]


def after(*values):
    return lax.optimization_barrier(values)


def turn_z(a, k):
    return lax.ppermute(a, ("z1", "z0"), [(i, (i + k) % 4) for i in range(4)])


def local(query_tokens, key_tokens, value_tokens, out_grad, fast_init):
    c = lax.axis_index("c")
    x = lax.axis_index(X)
    z1, z0 = lax.axis_index("z1"), lax.axis_index("z0")
    z = 2 * z1 + z0
    place = jnp.stack([c, x, z0, (z1 == c).astype(jnp.int32)]).astype(jnp.int32)
    eta = 0.25 / math.sqrt(D)

    def bound(kernel, *given):
        return lambda *refs: kernel(*given, *refs)

    first, held = pack_first(((0, 0), (1, 0)), place, fast_init, key_tokens, value_tokens)
    kv1 = exchange(first)
    (work,) = worked(first_weights_kernel, (), [], [], place, held, cross(held), far=["w0"])
    query_tokens, work = after(query_tokens, work)
    rest = pack(
        ((0, 1), (1, 1), (2, 1), (3, 1), (2, 0), (3, 0)), key_tokens, value_tokens, query_tokens, out_grad
    )

    rest, kv1 = after(rest, kv1)
    rest = exchange(rest)
    three = tok_scratch(3)
    send, keep, work = worked(
        first_update_kernel, work, SPLIT, [WP, FLAT], place, kv1,
        flops=6 * UNIT, near=["w0"], far=["k1", "v1", "s1", "p1", "q1", "r1", "fa1", "fb1", "hd1"],
    )
    chunk = scatter(place, send, keep)
    send, keep, work = worked(
        bound(next_update_kernel, eta), work, SPLIT, [WP, FLAT], place, rest, *gather(chunk),
        flops=6 * UNIT, near=["w0"], far=["w1", "g1", "k2", "v2", "s2", "p2", "q2", "r2", "fa2", "fb2", "hd2"],
    )
    (work,) = worked(
        first_readout_kernel, work, [], tok_scratch(2) + [WP] + three, rest, scalars=0,
        flops=8 * UNIT, near=["w1"], far=["sums", "dq1"],
    )
    chunk, work = after(scatter(place, send, keep), work)
    send, keep, work = worked(
        bound(last_readout_kernel, eta), work, SPLIT, three + [FLAT], place, rest, *gather(chunk),
        flops=6 * UNIT, near=["w1"], far=["w2", "g2", "da", "db"],
    )
    (work,) = worked(query_kernel, work, [], [], scalars=0, flops=2 * UNIT, near=["da", "db", "w2"], far=["dq2"])
    sum2, work = after(scatter(place, send, keep), work)
    send, keep, work = worked(
        bound(second_kernel, eta, False), work, SPLIT, [FLAT], place, *gather(sum2),
        flops=9 * UNIT, near=["g2", "sums", "k2", "v2", "s2", "p2", "q2", "r2"], far=["pp", "total", "ba", "bb", "be"],
    )
    back, work = worked(
        bound(token_kernel, False), work, [((PEERS, 4 * PACK, 128), BF)], [WP], scalars=0,
        flops=12 * UNIT, near=["pp", "fa2", "fb2", "hd2", "w1", "ba", "bb", "be", "dq1", "dq2"],
    )
    sum1, back, work = after(scatter(place, send, keep), back, work)
    send, keep, work = worked(
        bound(second_kernel, eta, True), work, SPLIT, [FLAT], place, *gather(sum1),
        flops=9 * UNIT, near=["g1", "total", "k1", "v1", "s1", "p1", "q1", "r1"], far=["pp", "ba", "bb", "be"],
    )
    last, work = worked(
        bound(token_kernel, True), work, [((PEERS, 6 * PACK, 128), BF)], [WP], back, scalars=0,
        flops=12 * UNIT, near=["pp", "fa1", "fb1", "hd1", "w0", "ba", "bb", "be"],
    )
    wide = ((2, ROWS, 16 * D), BF)
    out, last = after(scatter(place, send, keep, sum2, sum1), last)

    ring = jnp.stack([out, turn_z(out, 1), turn_z(out, 2), turn_z(out, 3)])
    ring, last = after(ring, last)
    last = exchange(last)

    def pick(core):
        return [lax.dynamic_index_in_dim(ring, (z - 2 * core - i) % 4, 0, keepdims=False) for i in range(2)]

    own, other = jnp.stack(pick(c)), jnp.stack(pick(1 - c))
    pair = jnp.concatenate([own, cross(other)])
    parts = [pair, turn(pair, 1), turn(pair, 2), turn(pair, 3)]
    (fast,) = call(
        fast_kernel, [((3, 2, D, D), F32)], place, *parts, scratch=[pltpu.VMEM((2, FULL, 128), F32)]
    )
    plan = [(0, 0, 5), (0, 1, 4), (1, 0, 0), (1, 1, 2), (2, 0, 1), (2, 1, 3)]
    query_grad, key_grad, value_grad = call(
        bound(unpack_kernel, [(out, block, 0, i * PACK) for out, block, i in plan], 1), [wide] * 3, last, scalars=0
    )
    return query_grad, key_grad, value_grad, fast


def solution(mesh):
    small = Mesh(mesh.devices.reshape((2,) * 7), EVERY)
    tokens = P(None, EVERY, None)
    fast = P(None, ("y1", "y0", "c"), None, None)
    return jax.shard_map(
        local,
        mesh=small,
        in_specs=(tokens, tokens, tokens, tokens, fast),
        out_specs=(tokens, tokens, tokens, fast),
        check_vma=False,
    )
```

```python
import math

import jax
import jax.numpy as jnp
from jax import lax
from jax.experimental import pallas as pl
from jax.experimental.pallas import tpu as pltpu
from jax.sharding import Mesh, PartitionSpec as P

BF = jnp.bfloat16
F32 = jnp.float32
EPS = 1e-06
D = 320
LANES = 128
MAT = 800
CHUNK = 304
HALF = 4 * CHUNK
FULL = 8 * CHUNK
ROWS = 32
PACK = 80
PEERS = 16
TOK = PEERS * ROWS
TILE = 128

X = ("x1", "x0")
C = ("c",)
YZ = ("y1", "y0", "z1", "z0")
EVERY = ("z1", "z0", "x1", "x0", "y1", "y0", "c")
ROOMY = pltpu.CompilerParams(vmem_limit_bytes=60 * 1024 * 1024)
PARAMS = pltpu.CompilerParams(vmem_limit_bytes=40 * 1024 * 1024)


def nn(a, b):
    return lax.dot_general(a, b, (((1,), (0,)), ((), ())), preferred_element_type=F32)


def nt(a, b):
    return lax.dot_general(a, b, (((1,), (1,)), ((), ())), preferred_element_type=F32)


def tn(a, b):
    return lax.dot_general(a, b, (((0,), (0,)), ((), ())), preferred_element_type=F32)


def put_tokens(out, head, off, rows):
    out[head, off : off + 32, :] = rows[:, 0:128]
    out[head, off + 32 : off + 64, :] = rows[:, 128:256]
    out[head, off + 64 : off + 80, :] = jnp.concatenate([rows[0:16, 256:320], rows[16:32, 256:320]], axis=1)


def get_tokens(ref, off, dst):
    dst[:, 0:128] = ref[:, off : off + 32, :].reshape(TOK, 128)
    dst[:, 128:256] = ref[:, off + 32 : off + 64, :].reshape(TOK, 128)
    tail = ref[:, off + 64 : off + 80, :]
    both = jnp.concatenate([tail[:, :, 0:64], tail[:, :, 64:128]], axis=1)
    dst[:, 256:320] = both.reshape(TOK, 64)


def put_token_grad(out, off, value):
    value = value.astype(BF)
    out[:, off : off + 32, :] = value[:, 0:128].reshape(PEERS, 32, 128)
    out[:, off + 32 : off + 64, :] = value[:, 128:256].reshape(PEERS, 32, 128)
    tail = value[:, 256:320].reshape(PEERS, 32, 64)
    out[:, off + 64 : off + 80, :] = jnp.concatenate([tail[:, 0:16, :], tail[:, 16:32, :]], axis=2)


def put_matrix(flat, which, m):
    base = which * MAT
    flat[base : base + 320, :] = m[:, 0:128]
    flat[base + 320 : base + 640, :] = m[:, 128:256]
    flat[base + 640 : base + 800, :] = jnp.concatenate([m[0:160, 256:320], m[160:320, 256:320]], axis=1)


def get_matrix(flat, which):
    base = which * MAT
    tail = flat[base + 640 : base + 800, :]
    last = jnp.concatenate([tail[:, 0:64], tail[:, 64:128]], axis=0)
    return jnp.concatenate([flat[base : base + 320, :], flat[base + 320 : base + 640, :], last], axis=1)


def clear_tail(flat):
    flat[3 * MAT : FULL, :] = jnp.zeros((FULL - 3 * MAT, 128), F32)


def split_out(flat, place, send, keep):
    core = place[0]
    send[...] = flat[pl.ds(pl.multiple_of((1 - core) * HALF, 16), HALF), :].astype(BF)
    keep[...] = flat[pl.ds(pl.multiple_of(core * HALF, 16), HALF), :]


def join_in(flat, place, parts):
    core, x = place[0], place[1]
    for k in range(4):
        at = lax.rem(x + 4 - k, 4) * CHUNK
        for half, part in ((core, parts[k]), (1 - core, parts[4 + k])):
            rows = pl.ds(pl.multiple_of(half * HALF + at, 16), CHUNK)
            flat[rows, :] = part[...].astype(F32)


def sigmoid(z):
    return 0.5 + 0.5 * jnp.tanh(0.5 * z)


def scale_of(g):
    return jnp.sqrt(jnp.sum(g * g) / (D * D) + EPS)


def rows_of(t):
    return pl.ds(pl.multiple_of(t * TILE, TILE), TILE)


def mat(ref, m):
    return ref[m * D : m * D + D, :]


def set_mat(ref, m, value):
    ref[m * D : m * D + D, :] = value


def set_halves(pair, m, w):
    high = w.astype(BF)
    set_mat(pair, m, high)
    set_mat(pair, 3 + m, (w - high.astype(F32)).astype(BF))


def nn2(a, pair, m):
    return nn(a, mat(pair, m)) + nn(a, mat(pair, 3 + m))


def nt2(a, pair, m):
    return nt(a, mat(pair, m)) + nt(a, mat(pair, 3 + m))


def over_tiles(step):
    def body(t, carry):
        step(rows_of(t))
        return carry

    lax.fori_loop(0, TOK // TILE, body, 0, unroll=True)


def update_body(moves, first, k, v, wp, s_out, p_out, q_out, r_out, f1, f3, hd, flat):
    def step(rows):
        kt, vt = k[rows, :], v[rows, :]
        z1, z3, e = nn2(kt, wp, 0), nn2(kt, wp, 1), -nt2(vt, wp, 2)
        sig = sigmoid(z1)
        s = z1 * sig
        rest = 1.0 - sig
        s1 = sig * (1.0 + z1 * rest)
        s2 = sig * rest * (2.0 + z1 * (1.0 - 2.0 * sig))
        p = z3 * s1
        s_out[rows, :] = s
        p_out[rows, :] = p
        q_out[rows, :] = e * s1
        r_out[rows, :] = e * z3 * s2
        f1[rows, :] = (e * p).astype(BF)
        f3[rows, :] = (e * s).astype(BF)
        hd[rows, :] = (s * z3).astype(BF)
        moves.flush_rows(first, rows)

    over_tiles(step)
    put_matrix(flat, 0, tn(k[...], f1[...]))
    put_matrix(flat, 1, tn(k[...], f3[...]))
    put_matrix(flat, 2, -tn(hd[...], v[...]))
    clear_tail(flat)


def readout_tiles(q, u, wp, d1, d3, td, ready=lambda rows: None):
    def step(rows):
        qt, ut = q[rows, :], u[rows, :]
        y1, y3, d = nn2(qt, wp, 0), nn2(qt, wp, 1), nt2(ut, wp, 2)
        sig = sigmoid(y1)
        s = y1 * sig
        s1 = sig * (1.0 + y1 * (1.0 - sig))
        d1[rows, :] = (d * y3 * s1).astype(BF)
        d3[rows, :] = (d * s).astype(BF)
        td[rows, :] = (s * y3).astype(BF)
        ready(rows)

    over_tiles(step)


def readout_sums(q, u, d1, d3, td):
    return tn(q[...], d1[...]), tn(q[...], d3[...]), tn(td[...], u[...])


def query_part(d1, d3, wp):
    return nt(d1[...], mat(wp, 0)) + nt(d3[...], mat(wp, 1))


def step_weights(w_old, flat, g_out, eta):
    for m in range(3):
        g = get_matrix(flat, m)
        set_mat(g_out, m, g.astype(BF))
        yield m, mat(w_old, m) - eta * (g / scale_of(g))


def first_weights_kernel(moves, place, held, got, w0):
    own = place[3] == 1
    for m in range(3):
        set_mat(w0, m, jnp.where(own, held[m], got[m]))


def first_update_kernel(moves, place, tokens, w0, send, keep, k, v, *refs):
    made, (wp, flat) = refs[:7], refs[7:]
    get_tokens(tokens, 0, k)
    get_tokens(tokens, PACK, v)
    moves.flush(2)
    moves.load()
    for m in range(3):
        set_halves(wp, m, mat(w0, m))
    update_body(moves, 2, k, v, wp, *made, flat)
    split_out(flat, place, send, keep)


def next_update_kernel(eta, moves, place, tokens, *refs):
    parts, (w0, send, keep, w1, g, k, v, *made, wp, flat) = refs[:8], refs[8:]
    join_in(flat, place, parts)
    get_tokens(tokens, 0, k)
    get_tokens(tokens, PACK, v)
    moves.load()
    for m, w in step_weights(w0, flat, g, eta):
        set_mat(w1, m, w)
        set_halves(wp, m, w)
    moves.flush(4)
    update_body(moves, 4, k, v, wp, *made, flat)
    split_out(flat, place, send, keep)


def first_readout_kernel(moves, tokens, w1, sums, grad, q, u, wp, d1, d3, td):
    moves.load()
    get_tokens(tokens, 4 * PACK, q)
    get_tokens(tokens, 5 * PACK, u)
    for m in range(3):
        set_halves(wp, m, mat(w1, m))
    readout_tiles(q, u, wp, d1, d3, td)
    for m, value in enumerate(readout_sums(q, u, d1, d3, td)):
        set_mat(sums, m, value)
    grad[...] = query_part(d1, d3, wp).astype(BF)


def last_readout_kernel(eta, moves, place, tokens, *refs):
    parts, (w1, send, keep, wp, g, d1, d3, q, u, td, flat) = refs[:8], refs[8:]
    join_in(flat, place, parts)
    get_tokens(tokens, 2 * PACK, q)
    get_tokens(tokens, 3 * PACK, u)
    moves.load()
    for m, w in step_weights(w1, flat, g, eta):
        set_halves(wp, m, w)
    moves.flush(2)
    readout_tiles(q, u, wp, d1, d3, td, lambda rows: moves.flush_rows(2, rows))
    for m, value in enumerate(readout_sums(q, u, d1, d3, td)):
        put_matrix(flat, m, value)
    clear_tail(flat)
    split_out(flat, place, send, keep)


def query_kernel(moves, d1, d3, wp, grad):
    moves.load()
    grad[...] = query_part(d1, d3, wp).astype(BF)


def second_kernel(eta, last, moves, place, *refs):
    parts, (g_in, extra, k, v, s_in, p_in, q_in, r_in, send, keep, pp, *refs) = refs[:8], refs[8:]
    total = None if last else refs[0]
    b1, b3, be, flat = refs[-4:]
    join_in(flat, place, parts)
    moves.load(2)
    for m in range(3):
        g = mat(g_in, m).astype(F32)
        p = get_matrix(flat, m)
        if last:
            p = p + mat(extra, m).astype(F32)
        else:
            set_mat(total, m, p.astype(BF))
        size = scale_of(g)
        along = jnp.sum(p * g) / (D * D * size * size * size)
        set_halves(pp, m, -eta * (p / size - g * along))
    done = 1 if last else 2
    moves.flush(done)
    moves.load()

    def step(rows):
        kt, vt = k[rows, :], v[rows, :]
        ba, bb, bh = nn2(kt, pp, 0), nn2(kt, pp, 1), -nt2(vt, pp, 2)
        s, p, q = s_in[rows, :], p_in[rows, :], q_in[rows, :]
        be[rows, :] = (bb * s + ba * p).astype(BF)
        b3[rows, :] = (ba * q + bh * s).astype(BF)
        b1[rows, :] = (ba * r_in[rows, :] + bb * q + bh * p).astype(BF)
        moves.flush_rows(done, rows)

    over_tiles(step)
    for m, value in enumerate((tn(k[...], b1[...]), tn(k[...], b3[...]), -tn(be[...], v[...]))):
        put_matrix(flat, m, value if last else value + mat(extra, m))
    clear_tail(flat)
    split_out(flat, place, send, keep)


def mix_kernel(place, keep, got, own, one, two, three):
    for k, out in enumerate((own, one, two, three)):
        rows = pl.ds(pl.multiple_of(lax.rem(place[1] + k, 4) * CHUNK, 16), CHUNK)
        out[...] = (keep[rows, :] + got[rows, :].astype(F32)).astype(out.dtype)


def add_kernel(*refs):
    total = refs[0][...].astype(F32)
    for ref in refs[1:-1]:
        total = total + ref[...].astype(F32)
    refs[-1][...] = total.astype(refs[-1].dtype)


def token_kernel(last, moves, *refs):
    if last:
        pp, f1, f3, hd, w, b1, b3, be, grad, wp = refs
    else:
        pp, f1, f3, hd, w, b1, b3, be, dq1, dq2, grad, wp = refs
    moves.load(4)
    key_part = nt2(f1[...], pp, 0) + nt2(f3[...], pp, 1)
    value_part = nn2(hd[...], pp, 2)
    moves.load()
    for m in range(3):
        set_halves(wp, m, mat(w, m))
    put_token_grad(grad, 0, key_part + nt2(b1[...], wp, 0) + nt2(b3[...], wp, 1))
    put_token_grad(grad, PACK, -(value_part + nn2(be[...], wp, 2)))
    if not last:
        put_token_grad(grad, 2 * PACK, dq2[...])
        put_token_grad(grad, 3 * PACK, dq1[...])


def fast_kernel(place, a0, a1, a2, a3, out, flat):
    core, x = place[0], place[1]
    for k, part in enumerate((a0, a1, a2, a3)):
        at = lax.rem(x + 4 - k, 4) * CHUNK
        for head in range(2):
            for i, half in enumerate((core, 1 - core)):
                rows = pl.ds(pl.multiple_of(half * HALF + at, 16), CHUNK)
                flat[head, rows, :] = part[2 * i + head].astype(F32)
    for head in range(2):
        for m in range(3):
            out[m, head] = get_matrix(flat.at[head], m)


VM = pl.BlockSpec(memory_space=pltpu.VMEM)
SM = pl.BlockSpec(memory_space=pltpu.SMEM)
HB = pl.BlockSpec(memory_space=pltpu.HBM)


def tok_scratch(n):
    return [pltpu.VMEM((TOK, D), BF) for _ in range(n)]


MATS = (3, D, D)


def layout(least, **sizes):
    places, at = {}, 0
    for name, rows in sizes.items():
        places[name] = (at, rows)
        at += rows
    return places, max(at, least)


WIDE, WIDE_ROWS = layout(
    20480, s1=TOK, p1=TOK, q1=TOK, r1=TOK, s2=TOK, p2=TOK, q2=TOK, r2=TOK, w0=3 * D, w1=3 * D, sums=3 * D
)
SHORT, SHORT_ROWS = layout(
    40960, k1=TOK, v1=TOK, fa1=TOK, fb1=TOK, hd1=TOK, k2=TOK, v2=TOK, fa2=TOK, fb2=TOK, hd2=TOK,
    g1=3 * D, g2=3 * D, total=3 * D, ba=TOK, bb=TOK, be=TOK, pp=6 * D, w2=6 * D, da=TOK, db=TOK, dq1=TOK, dq2=TOK,
)


def slot(name):
    return (0, *WIDE[name]) if name in WIDE else (1, *SHORT[name])


class Moves:
    def __init__(self, ins, outs, pieces):
        self.ins, self.outs, self.flushed, self.pieces, self.by_rows = ins, outs, 0, pieces, False
        for copy in ins:
            copy.start()

    def load(self, count=None):
        for copy in self.ins[:count]:
            copy.wait()
        self.ins = [] if count is None else self.ins[count:]

    def flush_rows(self, first, rows):
        self.by_rows = True
        for stage, there, sem in self.pieces[first:]:
            pltpu.make_async_copy(stage.at[rows, :], there.at[rows, :], sem).start()

    def flush(self, count=None):
        for copy in self.outs[self.flushed : count]:
            copy.start()
        self.flushed = len(self.outs) if count is None else count

    def end(self):
        if self.flushed < len(self.outs) and not self.by_rows:
            self.flush()
        for copy in self.outs:
            copy.wait()


def worked(kernel, work, outs, scratch, *args, scalars=1, flops=0, near=(), far=()):
    near, far = list(near), list(far)
    n_in, n_out, n_scratch, n_work = len(args), len(outs), len(scratch), len(work)

    def wrapped(*refs):
        args, refs = refs[:n_in], refs[n_in + n_work :]
        results, held, refs = refs[:n_out], refs[n_out : n_out + 2], refs[n_out + 2 :]
        own, stages, sems = refs[:n_scratch], refs[n_scratch:-1], refs[-1]
        ins, outs, pieces = [], [], []
        for i, name in enumerate(near + far):
            which, at, rows = slot(name)
            there = held[which].at[pl.ds(at, rows), :]
            if i < len(near):
                ins.append(pltpu.make_async_copy(there, stages[i], sems.at[i]))
            else:
                outs.append(pltpu.make_async_copy(stages[i], there, sems.at[i]))
                pieces.append((stages[i], there, sems.at[i]))
        moves = Moves(ins, outs, pieces)
        kernel(moves, *args, *stages[: len(near)], *results, *stages[len(near) :], *own)
        moves.end()

    stages = []
    for name in near + far:
        which, _, rows = slot(name)
        stages.append(pltpu.VMEM((rows, D), BF if which else F32))
    spaces = [jax.ShapeDtypeStruct((WIDE_ROWS, D), F32), jax.ShapeDtypeStruct((SHORT_ROWS, D), BF)]
    *results, wide, short = pl.pallas_call(
        wrapped,
        out_shape=[jax.ShapeDtypeStruct(s, t) for s, t in outs] + spaces,
        in_specs=[SM if i < scalars else VM for i in range(n_in)] + [HB] * n_work,
        out_specs=[VM] * n_out + [HB] * 2,
        scratch_shapes=list(scratch) + stages + [pltpu.SemaphoreType.DMA((len(stages),))],
        input_output_aliases={n_in + i: n_out + i for i in range(n_work)},
        compiler_params=PARAMS,
        cost_estimate=pl.CostEstimate(flops=flops, bytes_accessed=4_000_000, transcendentals=TOK * D),
    )(*args, *work)
    return *results, (wide, short)


def call(kernel, outs, *args, scalars=1, scratch=()):
    return pl.pallas_call(
        kernel,
        out_shape=[jax.ShapeDtypeStruct(s, t) for s, t in outs],
        in_specs=[SM if i < scalars else VM for i in range(len(args))],
        out_specs=[VM] * len(outs),
        scratch_shapes=list(scratch),
        compiler_params=PARAMS,
    )(*args)


def pack(plan, *args):
    def kernel(*refs):
        ins, out, stage, sems = refs[: len(args)], refs[-3], refs[-2], refs[-1]
        pack_pieces(plan, ins, out, stage, sems)

    n = len(plan)
    return pl.pallas_call(
        kernel,
        out_shape=jax.ShapeDtypeStruct((PEERS, n * PACK, 128), BF),
        in_specs=[HB] * len(args),
        out_specs=VM,
        scratch_shapes=[pltpu.VMEM((n, ROWS, 16 * D), BF), pltpu.SemaphoreType.DMA((n,))],
        compiler_params=ROOMY,
    )(*args)


def unpack(plan, n_out, *returned):
    n = len(plan)

    def kernel(*refs):
        sources, outs, (pieces, stage, sems) = refs[: len(returned)], refs[-3 - n_out : -3], refs[-3:]
        loads, stores = [], []
        for i, (source, place, which, block) in enumerate(plan):
            there = sources[source].at[:, pl.ds(place * PACK, PACK), :]
            loads.append(pltpu.make_async_copy(there, pieces.at[i], sems.at[i]))
            stores.append(pltpu.make_async_copy(stage.at[i], outs[which].at[block], sems.at[n + i]))
        for copy in loads:
            copy.start()
        for i in range(n):
            loads[i].wait()
            for head in range(16):
                tail = pieces[i, head, 64:80, :]
                last = jnp.concatenate([tail[:, 0:64], tail[:, 64:128]], axis=0)
                stage[i, :, head * D : head * D + D] = jnp.concatenate(
                    [pieces[i, head, 0:32, :], pieces[i, head, 32:64, :], last], axis=1
                )
            stores[i].start()
        for copy in stores:
            copy.wait()

    return pl.pallas_call(
        kernel,
        out_shape=[jax.ShapeDtypeStruct((2, ROWS, 16 * D), BF)] * n_out,
        in_specs=[HB] * len(returned),
        out_specs=[HB] * n_out,
        scratch_shapes=[
            pltpu.VMEM((n, PEERS, PACK, 128), BF),
            pltpu.VMEM((n, ROWS, 16 * D), BF),
            pltpu.SemaphoreType.DMA((2 * n,)),
        ],
        compiler_params=ROOMY,
    )(*returned)


def pack_pieces(plan, ins, out, stage, sems):
    copies = [
        pltpu.make_async_copy(ins[which].at[block], stage.at[i], sems.at[i]) for i, (which, block) in enumerate(plan)
    ]
    for copy in copies:
        copy.start()
    for i, copy in enumerate(copies):
        copy.wait()
        for head in range(16):
            put_tokens(out, head, i * PACK, stage[i, :, head * D : head * D + D])


def pack_first(plan, place, fast_init, *args):
    def kernel(place, given, *refs):
        ins, (out, held, stage, sems) = refs[: len(args)], refs[-4:]
        n = len(plan)
        weights = [pltpu.make_async_copy(given.at[m, place[2]], held.at[m], sems.at[n + m]) for m in range(3)]
        for copy in weights:
            copy.start()
        pack_pieces(plan, ins, out, stage, sems)
        for copy in weights:
            copy.wait()

    n = len(plan)
    return pl.pallas_call(
        kernel,
        out_shape=[jax.ShapeDtypeStruct((PEERS, n * PACK, 128), BF), jax.ShapeDtypeStruct(MATS, F32)],
        in_specs=[SM] + [HB] * (1 + len(args)),
        out_specs=[VM, VM],
        scratch_shapes=[pltpu.VMEM((n, ROWS, 16 * D), BF), pltpu.SemaphoreType.DMA((n + 3,))],
        compiler_params=ROOMY,
    )(place, fast_init, *args)


SPLIT = [((HALF, 128), BF), ((HALF, 128), F32)]
FLAT = pltpu.VMEM((FULL, 128), F32)
WP = pltpu.VMEM((6 * D, D), BF)
UNIT = 2 * TOK * D * D


def exchange(a):
    return lax.all_to_all(a, YZ, 0, 0, tiled=True)


def cross(a):
    return lax.ppermute(a, C, [(0, 1), (1, 0)])


def turn(a, k):
    return lax.ppermute(a, X, [(i, (i + k) % 4) for i in range(4)])


PIECE = (CHUNK, 128)


def scatter(place, send, keep, *more):
    own, *rest = call(mix_kernel, [(PIECE, F32)] + [(PIECE, BF)] * 3, place, keep, cross(send))
    got = [turn(part, k) for k, part in zip((1, 2, 3), rest)]
    (chunk,) = call(add_kernel, [(PIECE, BF)], own, *got, *more, scalars=0)
    return chunk


def gather(chunk):
    mine = [chunk, turn(chunk, 1), turn(chunk, 2), turn(chunk, 3)]
    return mine + [cross(part) for part in mine]


def after(*values):
    return lax.optimization_barrier(values)


def turn_z(a, k):
    return lax.ppermute(a, ("z1", "z0"), [(i, (i + k) % 4) for i in range(4)])


def local(query_tokens, key_tokens, value_tokens, out_grad, fast_init):
    c = lax.axis_index("c")
    x = lax.axis_index(X)
    z1, z0 = lax.axis_index("z1"), lax.axis_index("z0")
    z = 2 * z1 + z0
    place = jnp.stack([c, x, z0, (z1 == c).astype(jnp.int32)]).astype(jnp.int32)
    eta = 0.25 / math.sqrt(D)

    def bound(kernel, *given):
        return lambda *refs: kernel(*given, *refs)

    first, held = pack_first(((0, 0), (1, 0)), place, fast_init, key_tokens, value_tokens)
    kv1 = exchange(first)
    (work,) = worked(first_weights_kernel, (), [], [], place, held, cross(held), far=["w0"])
    query_tokens, work = after(query_tokens, work)
    rest = pack(
        ((0, 1), (1, 1), (2, 1), (3, 1), (2, 0), (3, 0)), key_tokens, value_tokens, query_tokens, out_grad
    )

    rest, kv1 = after(rest, kv1)
    rest = exchange(rest)
    three = tok_scratch(3)
    send, keep, work = worked(
        first_update_kernel, work, SPLIT, [WP, FLAT], place, kv1,
        flops=6 * UNIT, near=["w0"], far=["k1", "v1", "s1", "p1", "q1", "r1", "fa1", "fb1", "hd1"],
    )
    chunk = scatter(place, send, keep)
    send, keep, work = worked(
        bound(next_update_kernel, eta), work, SPLIT, [WP, FLAT], place, rest, *gather(chunk),
        flops=6 * UNIT, near=["w0"], far=["w1", "g1", "k2", "v2", "s2", "p2", "q2", "r2", "fa2", "fb2", "hd2"],
    )
    (work,) = worked(
        first_readout_kernel, work, [], tok_scratch(2) + [WP] + three, rest, scalars=0,
        flops=8 * UNIT, near=["w1"], far=["sums", "dq1"],
    )
    chunk, work = after(scatter(place, send, keep), work)
    send, keep, work = worked(
        bound(last_readout_kernel, eta), work, SPLIT, three + [FLAT], place, rest, *gather(chunk),
        flops=6 * UNIT, near=["w1"], far=["w2", "g2", "da", "db"],
    )
    (work,) = worked(query_kernel, work, [], [], scalars=0, flops=2 * UNIT, near=["da", "db", "w2"], far=["dq2"])
    sum2, work = after(scatter(place, send, keep), work)
    send, keep, work = worked(
        bound(second_kernel, eta, False), work, SPLIT, [FLAT], place, *gather(sum2),
        flops=9 * UNIT, near=["g2", "sums", "k2", "v2", "s2", "p2", "q2", "r2"], far=["pp", "total", "ba", "bb", "be"],
    )
    back, work = worked(
        bound(token_kernel, False), work, [((PEERS, 4 * PACK, 128), BF)], [WP], scalars=0,
        flops=12 * UNIT, near=["pp", "fa2", "fb2", "hd2", "w1", "ba", "bb", "be", "dq1", "dq2"],
    )
    sum1, back, work = after(scatter(place, send, keep), back, work)
    back = exchange(back)
    send, keep, work = worked(
        bound(second_kernel, eta, True), work, SPLIT, [FLAT], place, *gather(sum1),
        flops=9 * UNIT, near=["g1", "total", "k1", "v1", "s1", "p1", "q1", "r1"], far=["pp", "ba", "bb", "be"],
    )
    last, work = worked(
        bound(token_kernel, True), work, [((PEERS, 2 * PACK, 128), BF)], [WP], scalars=0,
        flops=12 * UNIT, near=["pp", "fa1", "fb1", "hd1", "w0", "ba", "bb", "be"],
    )
    out = scatter(place, send, keep, sum2, sum1)

    ring = jnp.stack([out, turn_z(out, 1), turn_z(out, 2), turn_z(out, 3)])
    ring, last, back = after(ring, last, back)
    last = exchange(last)

    def pick(core):
        return [lax.dynamic_index_in_dim(ring, (z - 2 * core - i) % 4, 0, keepdims=False) for i in range(2)]

    own, other = jnp.stack(pick(c)), jnp.stack(pick(1 - c))
    pair = jnp.concatenate([own, cross(other)])
    parts = [pair, turn(pair, 1), turn(pair, 2), turn(pair, 3)]
    (query_grad,) = unpack([(0, 2, 0, 1), (0, 3, 0, 0)], 1, back)
    plan = [(1, 0, 0, 1), (1, 1, 1, 1), (0, 0, 0, 0), (0, 1, 1, 0)]
    key_grad, value_grad = unpack(plan, 2, last, back)
    *parts, key_grad, value_grad = after(*parts, key_grad, value_grad)
    (fast,) = call(
        fast_kernel, [((3, 2, D, D), F32)], place, *parts, scratch=[pltpu.VMEM((2, FULL, 128), F32)]
    )
    return query_grad, key_grad, value_grad, fast


def solution(mesh):
    small = Mesh(mesh.devices.reshape((2,) * 7), EVERY)
    tokens = P(None, EVERY, None)
    fast = P(None, ("y1", "y0", "c"), None, None)
    return jax.shard_map(
        local,
        mesh=small,
        in_specs=(tokens, tokens, tokens, tokens, fast),
        out_specs=(tokens, tokens, tokens, fast),
        check_vma=False,
    )
```
